256 devices in a mesh: pair: 16 (over x, y), sib: 2 (over core), tile: 8 (over z).
Axes of the slice: x: 4, y: 4, z: 8, core: 2. Of those that a mesh axis runs over, the one named last changes fastest.
Arguments:
- children: float32 [32, 2, 2048, 2048], P('pair', 'sib', 'tile'), parts along dimension 0, may hold values from -2.2 to 2.2, as said below
Outputs:
- merged: float32 [32, 3072, 3072], P('pair', ('sib', 'tile')), parts along dimension 0
The draws below stay inside these ranges and needn't reach their ends.
There are 16 independent parts, one for each index of `pair`. The reference program is written for one: setup_inputs(seed, part) draws one part's arguments, and reference() takes and returns one part's arrays. A program takes and returns all parts, laid end to end along the dimension named above; each array names one. Nothing has to cross between parts.
Inputs may be any that keep to these rules, and one draw needn't show every extreme that they name: `children`: each map is symmetric, and the sum of a pair's two edge blocks is positive definite.
All inputs are finite; a program needn't handle non-finite values.
Results may differ from the reference program's by a relative error of at most 0.00007.
Values sent between devices are 32-bit elements; how exact they have to be, the bound alone decides.
No kernel may reach another device: no remote copies, remote signals or barrier semaphores. Data moves between devices by JAX's collectives and lax.ppermute only.
A program may use at most 128 MiB of HBM per device.

```python
import math
import jax
import jax.numpy as jnp
from jax import lax

EDGE = 512
PAIRS = 2
BOX = 2048
OUTER = 1536
MERGED = 3072
BLOCK = 256
OUT_BLK = 192
EDGE_BLK = 64
N_TILE = 8


def draw_children(key, part):
    key = jax.random.fold_in(key, 17)
    keys = jax.random.split(key, 5)
    index = jnp.arange(BOX, dtype=jnp.int32)
    block_id = index // BLOCK
    within = index % BLOCK
    is_edge = within >= OUT_BLK
    position = jnp.where(is_edge, EDGE_BLK * block_id + within - OUT_BLK, OUT_BLK * block_id + within)
    same_kind = is_edge[:, None] == is_edge[None, :]
    distance = jnp.abs(position[:, None] - position[None, :]).astype(jnp.float32)
    decay = jnp.where(distance < 1.5, 0.35, 0.1 * jnp.maximum(distance, 1.0) ** (-1.5))
    shape = (PAIRS, 2, BOX, BOX)
    signs = jnp.where(jax.random.bernoulli(keys[0], 0.5, shape), 1.0, -1.0)
    magnitude = jax.random.uniform(keys[1], shape, jnp.float32, 0.5, 1.0)
    banded = signs * magnitude * decay
    spread = 2.0 / math.sqrt(EDGE)
    mixed = jax.random.truncated_normal(keys[2], -4.0, 4.0, shape, jnp.float32) * spread
    diagonal = jax.random.uniform(keys[4], (PAIRS, 2, BOX), jnp.float32, 1.1, 2.2)
    base = jnp.where(same_kind, banded, mixed)
    upper = index[:, None] <= index[None, :]
    symmetric = jnp.where(upper, base, jnp.swapaxes(base, 2, 3))
    return jnp.where(index[:, None] == index[None, :], diagonal[..., :, None], symmetric)


def setup_inputs(seed: int = 0, part: int = 0) -> dict:
    key_list = jax.random.split(jax.random.key(seed), 2)
    part_splits = jax.random.split(jax.random.fold_in(key_list[1], part), 2)
    return {
        "children": draw_children(jax.random.fold_in(jax.random.fold_in(key_list[1], part), 71), part),
    }


def reference(children):
    layout = children.reshape(PAIRS, 2, N_TILE, BLOCK, N_TILE, BLOCK)
    outer_block = layout[:, :, :, :OUT_BLK, :, :OUT_BLK].reshape(PAIRS, 2, OUTER, OUTER)
    coupling_block = layout[:, :, :, :OUT_BLK, :, OUT_BLK:].reshape(PAIRS, 2, OUTER, EDGE)
    edge_block = layout[:, :, :, OUT_BLK:, :, OUT_BLK:].reshape(PAIRS, 2, EDGE, EDGE)
    schur_matrix = edge_block[:, 0] + edge_block[:, 1]
    factor = jnp.linalg.cholesky(schur_matrix)
    coupling = coupling_block.reshape(PAIRS, MERGED, EDGE)
    solved = lax.linalg.triangular_solve(factor, jnp.swapaxes(coupling, 1, 2), left_side=True, lower=True)
    schur_term = jnp.einsum('pkr,pkc->prc', solved, solved, precision=lax.Precision.HIGHEST)
    zeros_block = jnp.zeros((PAIRS, OUTER, OUTER), jnp.float32)
    upper_half = jnp.concatenate([outer_block[:, 0], zeros_block], axis=2)
    lower_half = jnp.concatenate([zeros_block, outer_block[:, 1]], axis=2)
    diagonal_part = jnp.concatenate([upper_half, lower_half], axis=1)
    return diagonal_part - schur_term
```

```python
import jax
import jax.numpy as jnp
from jax import lax
from jax.experimental import pallas as pl
from jax.experimental.pallas import tpu as pltpu
from jax.sharding import PartitionSpec as P

EDGE = 512
OUT_BLK = 192
EDGE_BLK = 64
N_TILE = 8
LANES = 128
F32 = jnp.float32
HIGHEST = lax.Precision.HIGHEST
VMEM_LIMIT = 48 * 1024 * 1024


def dot_full(a, b):
    return jnp.dot(a, b, precision=HIGHEST, preferred_element_type=F32)


def extract_kernel(place_ref, children_ref, coupling_ref, message_ref, tiles, sems):
    sib = place_ref[0]
    copies = []
    for pair in range(2):
        for block in range(N_TILE):
            copies.append(
                pltpu.make_async_copy(
                    children_ref.at[pair, :, pl.ds(256 * block + LANES, LANES)],
                    tiles.at[pair, block],
                    sems.at[pair, block],
                )
            )
    for copy in copies:
        copy.start()
    lane = lax.broadcasted_iota(jnp.int32, (256, LANES), 1)
    for pair in range(2):
        for half in range(N_TILE // 2):
            copies[pair * N_TILE + 2 * half].wait()
            copies[pair * N_TILE + 2 * half + 1].wait()
            first = pltpu.roll(tiles[pair, 2 * half], 64, 1)
            both = jnp.where(lane < 64, first, tiles[pair, 2 * half + 1])
            columns = pl.ds(LANES * half, LANES)
            coupling_ref[pair, :, columns] = both[:OUT_BLK]

            @pl.when(sib != pair)
            def _():
                message_ref[0:256, columns] = both

            @pl.when(sib == pair)
            def _():
                message_ref[256:320, columns] = both[OUT_BLK:]


def extract(place, children):
    return pl.pallas_call(
        extract_kernel,
        out_shape=[
            jax.ShapeDtypeStruct((2, OUT_BLK, EDGE), F32),
            jax.ShapeDtypeStruct((320, EDGE), F32),
        ],
        in_specs=[
            pl.BlockSpec(memory_space=pltpu.SMEM),
            pl.BlockSpec(memory_space=pl.ANY),
        ],
        out_specs=[pl.BlockSpec(memory_space=pltpu.VMEM)] * 2,
        scratch_shapes=[
            pltpu.VMEM((2, N_TILE, 256, LANES), F32),
            pltpu.SemaphoreType.DMA((2, N_TILE)),
        ],
        compiler_params=pltpu.CompilerParams(vmem_limit_bytes=VMEM_LIMIT),
        name="extract",
    )(place, children)


def along(x, k):
    return jnp.broadcast_to(x[:, k : k + 1], x.shape)


def down(x, a):
    return jnp.broadcast_to(x[a : a + 1, :], x.shape)


def inverse_128(rows):
    rows = list(rows)
    lane = lax.broadcasted_iota(jnp.int32, (8, LANES), 1)
    sublane = lax.broadcasted_iota(jnp.int32, (8, LANES), 0)
    for g in range(16):
        k = 8 * g
        pivot_rows = rows[g]
        spread = [along(pivot_rows, k + b) for b in range(8)]
        m = [[down(spread[b], a) for b in range(a + 1)] for a in range(8)]
        in_pivot = (lane >= k) & (lane < k + 8)
        r = [
            jnp.where(lane == k + a, -1.0, jnp.where(in_pivot, 0.0, down(pivot_rows, a)))
            for a in range(8)
        ]
        scale = [None] * 8
        low = [[None] * 8 for _ in range(8)]
        for c in range(8):
            scale[c] = 1.0 / m[c][c]
            for a in range(c + 1, 8):
                low[a][c] = m[a][c] * scale[c]
            for a in range(c + 1, 8):
                for b in range(c + 1, a + 1):
                    m[a][b] = m[a][b] - low[a][c] * m[b][c]
            for a in range(c + 1, 8):
                r[a] = r[a] - low[a][c] * r[c]
        q = [r[a] * scale[a] for a in range(8)]
        for c in range(7, -1, -1):
            for a in range(c):
                q[a] = q[a] - low[c][a] * q[c]
        for i in range(16):
            if i == g:
                continue
            old = rows[i]
            new = jnp.where(in_pivot, 0.0, old)
            for b in range(8):
                new = new - along(old, k + b) * q[b]
            rows[i] = new
        solved = q[0]
        for a in range(1, 8):
            solved = jnp.where(sublane == a, q[a], solved)
        rows[g] = solved
    return [-x for x in rows]


def weights_kernel(
    place_ref, own_ref, ring1_ref, ring2_ref, ring3_ref, ring4_ref, sibling_ref, coupling_ref, received_ref,
    own_weight_ref, sent_weight_ref, a_ref
):
    sib, tile = place_ref[0], place_ref[1]
    sign = 1 - 2 * sib

    def put(offset, value):
        position = lax.rem(tile + offset + 2 * N_TILE, N_TILE)
        a_ref[pl.ds(pl.multiple_of(position * EDGE_BLK, EDGE_BLK), EDGE_BLK), :] = value

    put(0, own_ref[...])
    put(-sign, ring1_ref[0])
    put(-2 * sign, ring2_ref[0])
    put(-3 * sign, ring3_ref[0])
    put(4, ring4_ref[...])
    for d in range(1, 4):
        put(d * sign, sibling_ref[d - 1])

    def step(j, _):
        base = pl.multiple_of(j * LANES, LANES)
        block = a_ref[pl.ds(base, LANES), pl.ds(base, LANES)]
        inverse = jnp.concatenate(inverse_128([block[8 * i : 8 * i + 8] for i in range(16)]), axis=0)
        columns = a_ref[:, pl.ds(base, LANES)]
        scaled_rows = dot_full(inverse, a_ref[pl.ds(base, LANES), :])
        scaled_columns = dot_full(columns, inverse)
        a_ref[...] = a_ref[...] - dot_full(columns, scaled_rows)
        a_ref[:, pl.ds(base, LANES)] = scaled_columns
        a_ref[pl.ds(base, LANES), :] = scaled_rows
        a_ref[pl.ds(base, LANES), pl.ds(base, LANES)] = -inverse
        return 0

    lax.fori_loop(0, EDGE // LANES, step, 0)
    negative_inverse = a_ref[...]
    own_weight_ref[...] = -dot_full(coupling_ref[sib], negative_inverse)
    sent_weight_ref[...] = -dot_full(received_ref[0:OUT_BLK], negative_inverse)


def weights(place, *operands):
    return pl.pallas_call(
        weights_kernel,
        out_shape=[jax.ShapeDtypeStruct((OUT_BLK, EDGE), F32)] * 2,
        in_specs=[pl.BlockSpec(memory_space=pltpu.SMEM)]
        + [pl.BlockSpec(memory_space=pltpu.VMEM)] * len(operands),
        out_specs=[pl.BlockSpec(memory_space=pltpu.VMEM)] * 2,
        scratch_shapes=[pltpu.VMEM((EDGE, EDGE), F32)],
        compiler_params=pltpu.CompilerParams(vmem_limit_bytes=VMEM_LIMIT),
        cost_estimate=pl.CostEstimate(flops=4_000_000_000, bytes_accessed=4_000_000, transcendentals=0),
        name="weights",
    )(place, *operands)


def split(x):
    high = x.astype(jnp.bfloat16)
    return high, (x - high.astype(F32)).astype(jnp.bfloat16)


def dot_rows(a, b):
    return lax.dot_general(a, b, (((1,), (1,)), ((), ())), preferred_element_type=F32)


def merge_kernel(place_ref, kept_ref, other_ref, gathered_ref, children_ref, out_ref, high, low):
    pair, step = pl.program_id(0), pl.program_id(1)
    sib = place_ref[0]

    @pl.when(step == 0)
    def _():
        weight = jnp.where(pair == sib, kept_ref[...], other_ref[...])
        high[...], low[...] = split(weight)

    points = gathered_ref[...].reshape(2 * OUT_BLK, EDGE)
    points_high, points_low = split(points)
    term = (
        dot_rows(low[...], points_high) + dot_rows(high[...], points_low)
    ) + dot_rows(high[...], points_high)
    out_ref[0] = -term

    @pl.when(step // 4 == sib)
    def _():
        own = children_ref[0]
        own = jnp.concatenate([own[:OUT_BLK, :OUT_BLK], own[:OUT_BLK, 256 : 256 + OUT_BLK]], axis=1)
        out_ref[0] = own - term


def merge(place, kept, other, gathered, children):
    return pl.pallas_call(
        merge_kernel,
        out_shape=jax.ShapeDtypeStruct((2, OUT_BLK, 2 * N_TILE * OUT_BLK), F32),
        grid_spec=pltpu.PrefetchScalarGridSpec(
            num_scalar_prefetch=1,
            grid=(2, N_TILE),
            in_specs=[
                pl.BlockSpec((OUT_BLK, EDGE), lambda p, j, place: (0, 0)),
                pl.BlockSpec((OUT_BLK, EDGE), lambda p, j, place: (0, 0)),
                pl.BlockSpec((2, 1, OUT_BLK, EDGE), lambda p, j, place: (j, p, 0, 0)),
                pl.BlockSpec((1, 256, 512), lambda p, j, place: (p, 0, jnp.clip(j - 4 * place[0], 0, 3))),
            ],
            out_specs=pl.BlockSpec((1, OUT_BLK, 2 * OUT_BLK), lambda p, j, place: (p, 0, j)),
            scratch_shapes=[pltpu.VMEM((OUT_BLK, EDGE), jnp.bfloat16)] * 2,
        ),
        compiler_params=pltpu.CompilerParams(vmem_limit_bytes=VMEM_LIMIT),
        name="merge",
    )(place, kept, other, gathered, children)


def shards(children):
    sib, tile = lax.axis_index("sib"), lax.axis_index("tile")
    place = jnp.stack([sib, tile]).astype(jnp.int32)
    children = children[:, 0]
    swap = [(0, 1), (1, 0)]
    around = [(t, (t + 1) % N_TILE) for t in range(N_TILE)]
    around += [(N_TILE + t, N_TILE + (t - 1) % N_TILE) for t in range(N_TILE)]

    coupling, message = extract(place, children)
    received = lax.ppermute(message, "sib", swap)
    gathered = lax.all_gather(coupling, ("sib", "tile"), axis=0)
    edges = jnp.stack([message[256:] + received[192:256], message[192:256] + received[256:]])
    ring1 = lax.ppermute(edges, ("sib", "tile"), around)
    ring2 = lax.ppermute(ring1, ("sib", "tile"), around)
    ring3 = lax.ppermute(ring2, ("sib", "tile"), around)
    ring4 = lax.ppermute(ring3[0], ("sib", "tile"), around)
    sibling = lax.ppermute(jnp.stack([ring1[1], ring2[1], ring3[1]]), "sib", swap)
    kept, sent = weights(place, edges[0], ring1, ring2, ring3, ring4, sibling, coupling, received)
    other = lax.ppermute(sent, "sib", swap)
    return merge(place, kept, other, gathered, children)


def solution(mesh):
    in_specs = (P("pair", "sib", "tile", None),)
    out_specs = P("pair", ("sib", "tile"), None)
    return jax.shard_map(shards, mesh=mesh, in_specs=in_specs, out_specs=out_specs, check_vma=False)
```

```python
import functools

import jax
import jax.numpy as jnp
from jax import lax
from jax.experimental import pallas as pl
from jax.experimental.pallas import tpu as pltpu
from jax.sharding import PartitionSpec as P

EDGE = 512
OUT_BLK = 192
EDGE_BLK = 64
N_TILE = 8
LANES = 128
F32 = jnp.float32
HIGHEST = lax.Precision.HIGHEST
PARAMS = pltpu.CompilerParams(vmem_limit_bytes=60 * 1024 * 1024)
SMEM = pl.BlockSpec(memory_space=pltpu.SMEM)
VMEM = pl.BlockSpec(memory_space=pltpu.VMEM)
HBM = pl.BlockSpec(memory_space=pl.ANY)


def dot_full(a, b):
    return jnp.dot(a, b, precision=HIGHEST, preferred_element_type=F32)


def split(x):
    high = x.astype(jnp.bfloat16)
    return high, (x - high.astype(F32)).astype(jnp.bfloat16)


def dot_split(a, b):
    a_high, a_low = split(a)
    b_high, b_low = split(b)
    low = jnp.dot(a_low, b_high, preferred_element_type=F32) + jnp.dot(a_high, b_low, preferred_element_type=F32)
    return low + jnp.dot(a_high, b_high, preferred_element_type=F32)


def extract_kernel(place_ref, children_ref, coupling_ref, edge_ref, tiles, sems):
    sib = place_ref[0]
    copies = []
    for pair in range(2):
        for block in range(N_TILE):
            copies.append(
                pltpu.make_async_copy(
                    children_ref.at[pair, :, pl.ds(256 * block + LANES, LANES)],
                    tiles.at[pair, block],
                    sems.at[pair, block],
                )
            )
    for copy in copies:
        copy.start()
    lane = lax.broadcasted_iota(jnp.int32, (256, LANES), 1)
    for pair in range(2):
        position = sib if pair == 0 else 1 - sib
        for half in range(N_TILE // 2):
            copies[pair * N_TILE + 2 * half].wait()
            copies[pair * N_TILE + 2 * half + 1].wait()
            first = pltpu.roll(tiles[pair, 2 * half], 64, 1)
            both = jnp.where(lane < 64, first, tiles[pair, 2 * half + 1])
            columns = pl.ds(LANES * half, LANES)
            coupling_ref[pair, :, columns] = both[:OUT_BLK]
            edge_ref[position, :, columns] = both[OUT_BLK:]


def extract(place, children):
    return pl.pallas_call(
        extract_kernel,
        out_shape=[
            jax.ShapeDtypeStruct((2, OUT_BLK, EDGE), F32),
            jax.ShapeDtypeStruct((2, EDGE_BLK, EDGE), F32),
        ],
        in_specs=[SMEM, HBM],
        out_specs=[VMEM, VMEM],
        scratch_shapes=[
            pltpu.VMEM((2, N_TILE, 256, LANES), F32),
            pltpu.SemaphoreType.DMA((2, N_TILE)),
        ],
        compiler_params=PARAMS,
        cost_estimate=pl.CostEstimate(flops=1000, bytes_accessed=1000, transcendentals=0),
        name="extract",
    )(place, children)


def along(x, k):
    return jnp.broadcast_to(x[:, k : k + 1], x.shape)


def down(x, a):
    return jnp.broadcast_to(x[a : a + 1, :], x.shape)


def inverse_128(rows):
    rows = list(rows)
    lane = lax.broadcasted_iota(jnp.int32, (8, LANES), 1)
    sublane = lax.broadcasted_iota(jnp.int32, (8, LANES), 0)
    for g in range(16):
        k = 8 * g
        pivot_rows = rows[g]
        spread = [along(pivot_rows, k + b) for b in range(8)]
        m = [[down(spread[b], a) for b in range(a + 1)] for a in range(8)]
        in_pivot = (lane >= k) & (lane < k + 8)
        r = [
            jnp.where(lane == k + a, -1.0, jnp.where(in_pivot, 0.0, down(pivot_rows, a)))
            for a in range(8)
        ]
        scale = [None] * 8
        low = [[None] * 8 for _ in range(8)]
        for c in range(8):
            scale[c] = 1.0 / m[c][c]
            for a in range(c + 1, 8):
                low[a][c] = m[a][c] * scale[c]
            for a in range(c + 1, 8):
                for b in range(c + 1, a + 1):
                    m[a][b] = m[a][b] - low[a][c] * m[b][c]
            for a in range(c + 1, 8):
                r[a] = r[a] - low[a][c] * r[c]
        q = [r[a] * scale[a] for a in range(8)]
        for c in range(7, -1, -1):
            for a in range(c):
                q[a] = q[a] - low[c][a] * q[c]
        for i in range(16):
            if i == g:
                continue
            old = rows[i]
            new = jnp.where(in_pivot, 0.0, old)
            for b in range(8):
                new = new - along(old, k + b) * q[b]
            rows[i] = new
        solved = q[0]
        for a in range(1, 8):
            solved = jnp.where(sublane == a, q[a], solved)
        rows[g] = solved
    return [-x for x in rows]


def block_of(tile, k):
    odd = lax.rem(tile, 2)
    toward = 1 - 2 * odd
    shift = [0, -toward, toward, 2][k]
    return lax.rem(lax.div(tile, 2) + shift + 4, 4)


def eliminate_kernel(k, place_ref, *refs):
    rows, panel = refs[-2:]
    sib, tile = place_ref[0], place_ref[1]
    odd = lax.rem(tile, 2)
    match = (sib + odd) != 1
    clash = (sib + odd) == 1

    def put(slot, value):
        rows[pl.ds(pl.multiple_of(slot * EDGE_BLK, EDGE_BLK), EDGE_BLK), :] = value

    def pick(ring, cross, own_way):
        return jnp.where(own_way, ring[0], cross[...])

    if k == 0:
        edges, ring1, cross1, state_out = refs[:-2]
        put(odd, edges[0])
        put(1 - odd, pick(ring1, cross1, match))
    elif k == 1:
        ring1, cross1, ring2, cross2, state_in, state_out = refs[:-2]
        put(odd, pick(ring2, cross2, clash))
        put(1 - odd, pick(ring1, cross1, clash))
    elif k == 2:
        ring2, cross2, ring3, cross3, state_in, state_out = refs[:-2]
        put(odd, pick(ring2, cross2, match))
        put(1 - odd, pick(ring3, cross3, match))
    else:
        ring3, cross3, last, state_in, part_ref, factor_ref, kept_ref, sent_ref = refs[:-2]
        put(odd, last[...])
        put(1 - odd, pick(ring3, cross3, clash))

    block = lax.broadcasted_iota(jnp.int32, (1, EDGE), 1) // LANES
    here = block_of(tile, k)
    columns = pl.ds(pl.multiple_of(here * LANES, LANES), LANES)
    if k == 0:
        panel[...] = rows[...]
    else:
        seen = block == block_of(tile, 0)
        for j in range(1, k):
            seen = seen | (block == block_of(tile, j))
        panel[...] = jnp.where(seen, 0.0, rows[...]) - dot_full(seen_columns(tile, k, rows), state_in[...])
    pivot = panel[:, columns]
    inverse = jnp.concatenate(inverse_128([pivot[8 * i : 8 * i + 8] for i in range(16)]), axis=0)
    row = lax.broadcasted_iota(jnp.int32, (LANES, LANES), 0)
    col = lax.broadcasted_iota(jnp.int32, (LANES, LANES), 1)
    panel[:, columns] = jnp.where(row == col, 1.0, 0.0)
    if k == 3:
        factor = dot_full(factor_ref[...], inverse)
        weights = part_ref[...] + dot_split(factor, panel[...])
        kept_ref[...] = weights[:OUT_BLK]
        sent_ref[...] = weights[OUT_BLK:]
        return
    scaled = dot_full(inverse, panel[...])
    if k > 0:
        done = k * LANES
        state_out[0:done] = jnp.where(block == here, 0.0, state_in[...]) - dot_full(state_in[:, columns], scaled)
    state_out[k * LANES : (k + 1) * LANES] = scaled


def seen_columns(tile, k, ref):
    parts = [ref[:, pl.ds(pl.multiple_of(block_of(tile, j) * LANES, LANES), LANES)] for j in range(k)]
    return jnp.concatenate(parts, axis=1)


def eliminate(k, place, *operands):
    if k < 3:
        out_shape = [jax.ShapeDtypeStruct(((k + 1) * LANES, EDGE), F32)]
    else:
        out_shape = [jax.ShapeDtypeStruct((OUT_BLK, EDGE), F32)] * 2
    return pl.pallas_call(
        functools.partial(eliminate_kernel, k),
        out_shape=out_shape,
        in_specs=[SMEM] + [VMEM] * len(operands),
        out_specs=[VMEM] * len(out_shape),
        scratch_shapes=[pltpu.VMEM((LANES, EDGE), F32)] * 2,
        compiler_params=PARAMS,
        cost_estimate=pl.CostEstimate(flops=1000, bytes_accessed=1000, transcendentals=0),
        name=f"eliminate{k}",
    )(place, *operands)


def part_kernel(place_ref, state_ref, coupling_ref, other_ref, part_ref, factor_ref):
    sib, tile = place_ref[0], place_ref[1]
    here = block_of(tile, 3)
    block = lax.broadcasted_iota(jnp.int32, (1, EDGE), 1) // LANES
    columns = pl.ds(pl.multiple_of(here * LANES, LANES), LANES)
    for i, ref in enumerate((coupling_ref.at[sib], other_ref.at[sib])):
        rows = pl.ds(i * OUT_BLK, OUT_BLK)
        part_ref[rows] = dot_split(seen_columns(tile, 3, ref), state_ref[...])
        factor_ref[rows] = ref[:, columns] - part_ref[rows, columns]
    part_ref[...] = jnp.where(block == here, 0.0, part_ref[...])


def part_weights(place, *operands):
    return pl.pallas_call(
        part_kernel,
        out_shape=[
            jax.ShapeDtypeStruct((2 * OUT_BLK, EDGE), F32),
            jax.ShapeDtypeStruct((2 * OUT_BLK, LANES), F32),
        ],
        in_specs=[SMEM] + [VMEM] * 3,
        out_specs=[VMEM] * 2,
        compiler_params=PARAMS,
        cost_estimate=pl.CostEstimate(flops=1000, bytes_accessed=1000, transcendentals=0),
        name="part_weights",
    )(place, *operands)


def dot_rows(a, b):
    return lax.dot_general(a, b, (((1,), (1,)), ((), ())), preferred_element_type=F32)


def merge_kernel(blocks, place_ref, kept_ref, other_ref, children_ref, *refs):
    out_ref, points, own, result, point_sems, own_sems, out_sems = refs[-7:]
    sources = list(refs[:-7])
    sib, tile = place_ref[0], place_ref[1]
    odd = lax.rem(tile, 2)
    match = (sib + odd) == 1

    def fetch(at, box, slot, pair, source):
        return pltpu.make_async_copy(
            source.at[pair],
            points.at[at, box, pair, pl.ds(pl.multiple_of(slot * OUT_BLK, OUT_BLK), OUT_BLK), :],
            point_sems.at[at, box, pair, slot],
        )

    def own_copy(at, pair):
        first = pl.multiple_of(512 * block_of(tile, blocks[at]), 512)
        return pltpu.make_async_copy(
            children_ref.at[pair, pl.ds(0, OUT_BLK), pl.ds(first, 512)], own.at[at, pair], own_sems.at[at, pair]
        )

    for at, k in enumerate(blocks):
        for box in range(2):
            choices = [sources.pop(0) for _ in range(4 if k in (1, 2) else 3)]
            choices = [choices[:-2], choices[-2:]]
            for pair in range(2):
                for slot, candidates in ((odd, choices[0]), (1 - odd, choices[1])):
                    if len(candidates) == 1:
                        fetch(at, box, slot, pair, candidates[0]).start()
                    else:

                        @pl.when(match)
                        def _():
                            fetch(at, box, slot, pair, candidates[0]).start()

                        @pl.when(jnp.logical_not(match))
                        def _():
                            fetch(at, box, slot, pair, candidates[1]).start()

                if box == 0:
                    own_copy(at, pair).start()

    weights = [split(jnp.where(sib == pair, kept_ref[...], other_ref[...])) for pair in range(2)]
    writes = []
    for at, k in enumerate(blocks):
        for box in range(2):
            for pair in range(2):
                weight_high, weight_low = weights[pair]
                for slot in range(2):
                    fetch(at, box, slot, pair, refs[0]).wait()
                points_high, points_low = split(points[at, box, pair])
                both = dot_rows(jnp.concatenate([weight_high, weight_low], axis=0), points_high)
                term = (both[OUT_BLK:] + dot_rows(weight_high, points_low)) + both[:OUT_BLK]
                if box == 0:
                    own_copy(at, pair).wait()
                    diagonal = own[at, pair]
                    term = term - jnp.concatenate([diagonal[:, :OUT_BLK], diagonal[:, 256 : 256 + OUT_BLK]], axis=1)
                result[at, box, pair] = -term
                which = sib if box == 0 else 1 - sib
                columns = pl.multiple_of((4 * which + block_of(tile, k)) * 2 * OUT_BLK, 2 * OUT_BLK)
                write = pltpu.make_async_copy(
                    result.at[at, box, pair],
                    out_ref.at[pair, :, pl.ds(columns, 2 * OUT_BLK)],
                    out_sems.at[at, box, pair],
                )
                write.start()
                writes.append(write)
    for write in writes:
        write.wait()


def merge(blocks, place, kept, other, children, sources, out):
    operands = [place, kept, other, children, *sources]
    specs = [SMEM, VMEM, VMEM] + [HBM] * (1 + len(sources))
    aliases = {}
    if out is not None:
        aliases = {len(operands): 0}
        operands.append(out)
        specs.append(HBM)
    n = len(blocks)
    return pl.pallas_call(
        functools.partial(merge_kernel, blocks),
        out_shape=jax.ShapeDtypeStruct((2, OUT_BLK, 2 * N_TILE * OUT_BLK), F32),
        in_specs=specs,
        out_specs=HBM,
        scratch_shapes=[
            pltpu.VMEM((n, 2, 2, 2 * OUT_BLK, EDGE), F32),
            pltpu.VMEM((n, 2, OUT_BLK, 512), F32),
            pltpu.VMEM((n, 2, 2, OUT_BLK, 2 * OUT_BLK), F32),
            pltpu.SemaphoreType.DMA((n, 2, 2, 2)),
            pltpu.SemaphoreType.DMA((n, 2)),
            pltpu.SemaphoreType.DMA((n, 2, 2)),
        ],
        input_output_aliases=aliases,
        compiler_params=PARAMS,
        cost_estimate=pl.CostEstimate(flops=1000, bytes_accessed=1000, transcendentals=0),
        name="merge" + "".join(map(str, blocks)),
    )(*operands)


def tie(*arrays):
    return lax.optimization_barrier(arrays)


def shards(children):
    sib, tile = lax.axis_index("sib"), lax.axis_index("tile")
    place = jnp.stack([sib, tile]).astype(jnp.int32)
    children = children[:, 0]
    around = [(t, (t + 1) % N_TILE) for t in range(N_TILE)]
    around += [(N_TILE + t, N_TILE + (t - 1) % N_TILE) for t in range(N_TILE)]
    against = [(to, source) for source, to in around]

    def swap(x):
        return lax.ppermute(x, "sib", [(0, 1), (1, 0)])

    def pass_on(x):
        return lax.ppermute(x, ("sib", "tile"), around)

    def pass_edges(x):
        return lax.ppermute(x, ("sib", "tile"), against)

    coupling, edge = extract(place, children)
    edges = edge + swap(edge)[::-1]
    own_box = [coupling, pass_on(coupling)]
    other_box = [swap(coupling)]
    other_box.append(pass_on(other_box[0]))
    ring, cross = [edges, pass_edges(edges)], [None]
    ring.append(pass_edges(ring[1]))
    cross.append(swap(ring[1][1]))
    cross[1], own_box[1] = tie(cross[1], own_box[1])
    own_box.append(pass_on(own_box[1]))
    state = eliminate(0, place, edges, ring[1], cross[1])[0]
    state, ring[2], other_box[1] = tie(state, ring[2], other_box[1])
    ring.append(pass_edges(ring[2]))
    cross.append(swap(ring[2][1]))
    other_box.append(pass_on(other_box[1]))
    state = eliminate(1, place, ring[1], cross[1], ring[2], cross[2], state)[0]
    state, ring[3], own_box[2] = tie(state, ring[3], own_box[2])
    last = pass_edges(ring[3][0])
    cross.append(swap(ring[3][1]))
    own_box.append(pass_on(own_box[2]))
    state = eliminate(2, place, ring[2], cross[2], ring[3], cross[3], state)[0]
    state, last, other_box[2] = tie(state, last, other_box[2])
    other_box.append(pass_on(other_box[2]))
    part, factor = part_weights(place, state, coupling, other_box[0])
    part, own_box[3] = tie(part, own_box[3])
    own_box.append(pass_on(own_box[3]))
    kept, sent = eliminate(3, place, ring[3], cross[3], last, state, part, factor)
    other = swap(sent)
    own_cross = [None] + [swap(own_box[d]) for d in range(1, 4)]
    other_cross = [None] + [swap(other_box[d]) for d in range(1, 4)]

    mine = [own_box, other_box]
    theirs = [other_cross, own_cross]
    zero = [coupling, other_box[0]]
    sources = [[], [], [], []]
    for b in range(2):
        sources[0] += [zero[b], mine[b][1], theirs[b][1]]
        sources[1] += [theirs[b][2], mine[b][2], theirs[b][1], mine[b][1]]
    out = merge((0, 1), place, kept, other, children, sources[0] + sources[1], None)
    out, own_box[4] = tie(out, own_box[4])
    four = [own_box[4], swap(own_box[4])]
    for b in range(2):
        sources[2] += [mine[b][2], theirs[b][2], mine[b][3], theirs[b][3]]
        sources[3] += [four[b], theirs[b][3], mine[b][3]]
    return merge((2, 3), place, kept, other, children, sources[2] + sources[3], out)


def solution(mesh):
    in_specs = (P("pair", "sib", "tile", None),)
    out_specs = P("pair", ("sib", "tile"), None)
    return jax.shard_map(shards, mesh=mesh, in_specs=in_specs, out_specs=out_specs, check_vma=False)
```

```python
import functools

import jax
import jax.numpy as jnp
from jax import lax
from jax.experimental import pallas as pl
from jax.experimental.pallas import tpu as pltpu
from jax.sharding import PartitionSpec as P

EDGE = 512
OUT_BLK = 192
EDGE_BLK = 64
N_TILE = 8
LANES = 128
F32 = jnp.float32
HIGHEST = lax.Precision.HIGHEST
PARAMS = pltpu.CompilerParams(vmem_limit_bytes=60 * 1024 * 1024)
SMEM = pl.BlockSpec(memory_space=pltpu.SMEM)
VMEM = pl.BlockSpec(memory_space=pltpu.VMEM)
HBM = pl.BlockSpec(memory_space=pl.ANY)


def dot_full(a, b):
    return jnp.dot(a, b, precision=HIGHEST, preferred_element_type=F32)


def split(x):
    high = x.astype(jnp.bfloat16)
    return high, (x - high.astype(F32)).astype(jnp.bfloat16)


def dot_split(a, b):
    a_high, a_low = split(a)
    b_high, b_low = split(b)
    low = jnp.dot(a_low, b_high, preferred_element_type=F32) + jnp.dot(a_high, b_low, preferred_element_type=F32)
    return low + jnp.dot(a_high, b_high, preferred_element_type=F32)


def extract_kernel(place_ref, children_ref, coupling_ref, edge_ref, tiles, sems):
    sib = place_ref[0]
    copies = []
    for pair in range(2):
        for block in range(N_TILE):
            copies.append(
                pltpu.make_async_copy(
                    children_ref.at[pair, :, pl.ds(256 * block + LANES, LANES)],
                    tiles.at[pair, block],
                    sems.at[pair, block],
                )
            )
    for copy in copies:
        copy.start()
    lane = lax.broadcasted_iota(jnp.int32, (256, LANES), 1)
    for pair in range(2):
        position = sib if pair == 0 else 1 - sib
        for half in range(N_TILE // 2):
            copies[pair * N_TILE + 2 * half].wait()
            copies[pair * N_TILE + 2 * half + 1].wait()
            first = pltpu.roll(tiles[pair, 2 * half], 64, 1)
            both = jnp.where(lane < 64, first, tiles[pair, 2 * half + 1])
            columns = pl.ds(LANES * half, LANES)
            coupling_ref[pair, :, columns] = both[:OUT_BLK]
            edge_ref[position, :, columns] = both[OUT_BLK:]


def extract(place, children):
    return pl.pallas_call(
        extract_kernel,
        out_shape=[
            jax.ShapeDtypeStruct((2, OUT_BLK, EDGE), F32),
            jax.ShapeDtypeStruct((2, EDGE_BLK, EDGE), F32),
        ],
        in_specs=[SMEM, HBM],
        out_specs=[VMEM, VMEM],
        scratch_shapes=[
            pltpu.VMEM((2, N_TILE, 256, LANES), F32),
            pltpu.SemaphoreType.DMA((2, N_TILE)),
        ],
        compiler_params=PARAMS,
        cost_estimate=pl.CostEstimate(flops=1000, bytes_accessed=1000, transcendentals=0),
        name="extract",
    )(place, children)


def along(x, k):
    return jnp.broadcast_to(x[:, k : k + 1], x.shape)


def down(x, a):
    return jnp.broadcast_to(x[a : a + 1, :], x.shape)


def inverse_128(rows):
    rows = list(rows)
    lane = lax.broadcasted_iota(jnp.int32, (8, LANES), 1)
    sublane = lax.broadcasted_iota(jnp.int32, (8, LANES), 0)
    for g in range(16):
        k = 8 * g
        pivot_rows = rows[g]
        spread = [along(pivot_rows, k + b) for b in range(8)]
        m = [[down(spread[b], a) for b in range(a + 1)] for a in range(8)]
        in_pivot = (lane >= k) & (lane < k + 8)
        r = [
            jnp.where(lane == k + a, -1.0, jnp.where(in_pivot, 0.0, down(pivot_rows, a)))
            for a in range(8)
        ]
        scale = [None] * 8
        low = [[None] * 8 for _ in range(8)]
        for c in range(8):
            scale[c] = 1.0 / m[c][c]
            for a in range(c + 1, 8):
                low[a][c] = m[a][c] * scale[c]
            for a in range(c + 1, 8):
                for b in range(c + 1, a + 1):
                    m[a][b] = m[a][b] - low[a][c] * m[b][c]
            for a in range(c + 1, 8):
                r[a] = r[a] - low[a][c] * r[c]
        q = [r[a] * scale[a] for a in range(8)]
        for c in range(7, -1, -1):
            for a in range(c):
                q[a] = q[a] - low[c][a] * q[c]
        for i in range(16):
            if i == g:
                continue
            old = rows[i]
            new = jnp.where(in_pivot, 0.0, old)
            for b in range(8):
                new = new - along(old, k + b) * q[b]
            rows[i] = new
        solved = q[0]
        for a in range(1, 8):
            solved = jnp.where(sublane == a, q[a], solved)
        rows[g] = solved
    return [-x for x in rows]


def block_of(tile, k):
    odd = lax.rem(tile, 2)
    toward = 1 - 2 * odd
    shift = [0, -toward, toward, 2][k]
    return lax.rem(lax.div(tile, 2) + shift + 4, 4)


def seen_columns(tile, k, ref):
    parts = [ref[:, pl.ds(pl.multiple_of(block_of(tile, j) * LANES, LANES), LANES)] for j in range(k)]
    return jnp.concatenate(parts, axis=1)


def border(tile, k, rows, panel, state_in, state_out):
    block = lax.broadcasted_iota(jnp.int32, (1, EDGE), 1) // LANES
    here = block_of(tile, k)
    columns = pl.ds(pl.multiple_of(here * LANES, LANES), LANES)
    done = k * LANES
    if k == 0:
        panel[...] = rows[...]
    else:
        seen = block == block_of(tile, 0)
        for j in range(1, k):
            seen = seen | (block == block_of(tile, j))
        known = state_in[0:done]
        panel[...] = jnp.where(seen, 0.0, rows[...]) - dot_full(seen_columns(tile, k, rows), known)
    pivot = panel[:, columns]
    inverse = jnp.concatenate(inverse_128([pivot[8 * i : 8 * i + 8] for i in range(16)]), axis=0)
    row = lax.broadcasted_iota(jnp.int32, (LANES, LANES), 0)
    col = lax.broadcasted_iota(jnp.int32, (LANES, LANES), 1)
    panel[:, columns] = jnp.where(row == col, 1.0, 0.0)
    if state_out is None:
        return inverse
    scaled = dot_full(inverse, panel[...])
    if k > 0:
        before = state_in[0:done, columns]
        state_out[0:done] = jnp.where(block == here, 0.0, state_in[0:done]) - dot_full(before, scaled)
    state_out[done : done + LANES] = scaled
    return inverse


def put_rows(rows, odd, first, second):
    rows[pl.ds(pl.multiple_of(odd * EDGE_BLK, EDGE_BLK), EDGE_BLK), :] = first
    rows[pl.ds(pl.multiple_of((1 - odd) * EDGE_BLK, EDGE_BLK), EDGE_BLK), :] = second


def pick(ring, cross, own_way):
    return jnp.where(own_way, ring[0], cross[...])


def first_kernel(place_ref, edges, ring1, cross1, state, rows, panel):
    sib, tile = place_ref[0], place_ref[1]
    odd = lax.rem(tile, 2)
    put_rows(rows, odd, edges[0], pick(ring1, cross1, (sib + odd) != 1))
    border(tile, 0, rows, panel, None, state)


def next_kernel(place_ref, ring1, cross1, ring2, cross2, state_in, state, rows, panel):
    sib, tile = place_ref[0], place_ref[1]
    odd = lax.rem(tile, 2)
    clash = (sib + odd) == 1
    put_rows(rows, odd, pick(ring2, cross2, clash), pick(ring1, cross1, clash))
    border(tile, 1, rows, panel, state_in, state)


def second_kernel(
    place_ref, ring2, cross2, ring3, cross3, last, state_in, coupling, other, kept, sent, rows, panel, state, part
):
    sib, tile = place_ref[0], place_ref[1]
    odd = lax.rem(tile, 2)
    match, clash = (sib + odd) != 1, (sib + odd) == 1
    put_rows(rows, odd, pick(ring2, cross2, match), pick(ring3, cross3, match))
    border(tile, 2, rows, panel, state_in, state)
    block = lax.broadcasted_iota(jnp.int32, (1, EDGE), 1) // LANES
    here = block_of(tile, 3)
    columns = pl.ds(pl.multiple_of(here * LANES, LANES), LANES)
    put_rows(rows, odd, last[...], pick(ring3, cross3, clash))
    for i, ref in enumerate((coupling.at[sib], other.at[sib])):
        part[i * OUT_BLK : (i + 1) * OUT_BLK] = dot_split(seen_columns(tile, 3, ref), state[...])
    inverse = border(tile, 3, rows, panel, state, None)
    for i, (ref, out) in enumerate(((coupling.at[sib], kept), (other.at[sib], sent))):
        mine = pl.ds(i * OUT_BLK, OUT_BLK)
        factor = dot_full(ref[:, columns] - part[mine, columns], inverse)
        out[...] = jnp.where(block == here, 0.0, part[mine]) + dot_split(factor, panel[...])


def eliminate(k, place, *operands):
    return pl.pallas_call(
        (first_kernel, next_kernel)[k],
        out_shape=jax.ShapeDtypeStruct(((k + 1) * LANES, EDGE), F32),
        in_specs=[SMEM] + [VMEM] * len(operands),
        out_specs=VMEM,
        scratch_shapes=[pltpu.VMEM((LANES, EDGE), F32)] * 2,
        compiler_params=PARAMS,
        name=f"eliminate{k}",
    )(place, *operands)


def eliminate_second(place, *operands):
    return pl.pallas_call(
        second_kernel,
        out_shape=[jax.ShapeDtypeStruct((OUT_BLK, EDGE), F32)] * 2,
        in_specs=[SMEM] + [VMEM] * len(operands),
        out_specs=[VMEM] * 2,
        scratch_shapes=[pltpu.VMEM((LANES, EDGE), F32)] * 2
        + [pltpu.VMEM((3 * LANES, EDGE), F32), pltpu.VMEM((2 * OUT_BLK, EDGE), F32)],
        compiler_params=PARAMS,
        name="eliminate_second",
    )(place, *operands)


def dot_rows(a, b):
    return lax.dot_general(a, b, (((1,), (1,)), ((), ())), preferred_element_type=F32)


def merge_kernel(blocks, place_ref, kept_ref, other_ref, children_ref, *refs):
    out_ref, points, own, result, point_sems, own_sems, out_sems = refs[-7:]
    sources = list(refs[:-7])
    sib, tile = place_ref[0], place_ref[1]
    odd = lax.rem(tile, 2)
    match = (sib + odd) == 1

    def fetch(at, box, slot, pair, source):
        return pltpu.make_async_copy(
            source.at[pair],
            points.at[at, box, pair, pl.ds(pl.multiple_of(slot * OUT_BLK, OUT_BLK), OUT_BLK), :],
            point_sems.at[at, box, pair, slot],
        )

    def own_copy(at, pair):
        first = pl.multiple_of(512 * block_of(tile, blocks[at]), 512)
        return pltpu.make_async_copy(
            children_ref.at[pair, pl.ds(0, OUT_BLK), pl.ds(first, 512)], own.at[at, pair], own_sems.at[at, pair]
        )

    for at, k in enumerate(blocks):
        for box in range(2):
            choices = [sources.pop(0) for _ in range(4 if k in (1, 2) else 3)]
            choices = [choices[:-2], choices[-2:]]
            for pair in range(2):
                for slot, candidates in ((odd, choices[0]), (1 - odd, choices[1])):
                    if len(candidates) == 1:
                        fetch(at, box, slot, pair, candidates[0]).start()
                    else:

                        @pl.when(match)
                        def _():
                            fetch(at, box, slot, pair, candidates[0]).start()

                        @pl.when(jnp.logical_not(match))
                        def _():
                            fetch(at, box, slot, pair, candidates[1]).start()

                if box == 0:
                    own_copy(at, pair).start()

    weights = [split(jnp.where(sib == pair, kept_ref[...], other_ref[...])) for pair in range(2)]
    writes = []
    for at, k in enumerate(blocks):
        for box in range(2):
            for pair in range(2):
                weight_high, weight_low = weights[pair]
                for slot in range(2):
                    fetch(at, box, slot, pair, refs[0]).wait()
                points_high, points_low = split(points[at, box, pair])
                both = dot_rows(jnp.concatenate([weight_high, weight_low], axis=0), points_high)
                term = (both[OUT_BLK:] + dot_rows(weight_high, points_low)) + both[:OUT_BLK]
                if box == 0:
                    own_copy(at, pair).wait()
                    diagonal = own[at, pair]
                    term = term - jnp.concatenate([diagonal[:, :OUT_BLK], diagonal[:, 256 : 256 + OUT_BLK]], axis=1)
                result[at, box, pair] = -term
                which = sib if box == 0 else 1 - sib
                columns = pl.multiple_of((4 * which + block_of(tile, k)) * 2 * OUT_BLK, 2 * OUT_BLK)
                write = pltpu.make_async_copy(
                    result.at[at, box, pair],
                    out_ref.at[pair, :, pl.ds(columns, 2 * OUT_BLK)],
                    out_sems.at[at, box, pair],
                )
                write.start()
                writes.append(write)
    for write in writes:
        write.wait()


def merge(blocks, place, kept, other, children, sources, out):
    operands = [place, kept, other, children, *sources]
    specs = [SMEM, VMEM, VMEM] + [HBM] * (1 + len(sources))
    aliases = {}
    if out is not None:
        aliases = {len(operands): 0}
        operands.append(out)
        specs.append(HBM)
    n = len(blocks)
    return pl.pallas_call(
        functools.partial(merge_kernel, blocks),
        out_shape=jax.ShapeDtypeStruct((2, OUT_BLK, 2 * N_TILE * OUT_BLK), F32),
        in_specs=specs,
        out_specs=HBM,
        scratch_shapes=[
            pltpu.VMEM((n, 2, 2, 2 * OUT_BLK, EDGE), F32),
            pltpu.VMEM((n, 2, OUT_BLK, 512), F32),
            pltpu.VMEM((n, 2, 2, OUT_BLK, 2 * OUT_BLK), F32),
            pltpu.SemaphoreType.DMA((n, 2, 2, 2)),
            pltpu.SemaphoreType.DMA((n, 2)),
            pltpu.SemaphoreType.DMA((n, 2, 2)),
        ],
        input_output_aliases=aliases,
        compiler_params=PARAMS,
        cost_estimate=pl.CostEstimate(flops=1000, bytes_accessed=1000, transcendentals=0),
        name="merge" + "".join(map(str, blocks)),
    )(*operands)


def tie(*arrays):
    return lax.optimization_barrier(arrays)


def shards(children):
    sib, tile = lax.axis_index("sib"), lax.axis_index("tile")
    place = jnp.stack([sib, tile]).astype(jnp.int32)
    children = children[:, 0]
    around = [(t, (t + 1) % N_TILE) for t in range(N_TILE)]
    around += [(N_TILE + t, N_TILE + (t - 1) % N_TILE) for t in range(N_TILE)]
    against = [(to, source) for source, to in around]

    def swap(x):
        return lax.ppermute(x, "sib", [(0, 1), (1, 0)])

    def pass_on(x):
        return lax.ppermute(x, ("sib", "tile"), around)

    def pass_edges(x):
        return lax.ppermute(x, ("sib", "tile"), against)

    coupling, edge = extract(place, children)
    edges = edge + swap(edge)[::-1]
    own_box = [coupling, pass_on(coupling)]
    other_box = [swap(coupling)]
    other_box.append(pass_on(other_box[0]))
    ring, cross = [edges, pass_edges(edges)], [None]
    ring.append(pass_edges(ring[1]))
    cross.append(swap(ring[1][1]))
    cross[1], own_box[1] = tie(cross[1], own_box[1])
    own_box.append(pass_on(own_box[1]))
    state = eliminate(0, place, edges, ring[1], cross[1])
    state, ring[2], other_box[1] = tie(state, ring[2], other_box[1])
    ring.append(pass_edges(ring[2]))
    cross.append(swap(ring[2][1]))
    other_box.append(pass_on(other_box[1]))
    state = eliminate(1, place, ring[1], cross[1], ring[2], cross[2], state)
    state, ring[3], own_box[2] = tie(state, ring[3], own_box[2])
    last = pass_edges(ring[3][0])
    cross.append(swap(ring[3][1]))
    own_box.append(pass_on(own_box[2]))
    last, own_box[3], other_box[2] = tie(last, own_box[3], other_box[2])
    own_box.append(pass_on(own_box[3]))
    other_box.append(pass_on(other_box[2]))
    kept, sent = eliminate_second(place, ring[2], cross[2], ring[3], cross[3], last, state, coupling, other_box[0])
    kept, sent, own_box[4], other_box[3] = tie(kept, sent, own_box[4], other_box[3])
    other = swap(sent)
    own_cross = [None] + [swap(own_box[d]) for d in range(1, 5)]
    other_cross = [None] + [swap(other_box[d]) for d in range(1, 4)]

    mine = [own_box, other_box]
    theirs = [other_cross, own_cross]
    zero = [coupling, other_box[0]]
    four = [own_box[4], own_cross[4]]
    sources = [[], [], [], []]
    for b in range(2):
        sources[0] += [zero[b], mine[b][1], theirs[b][1]]
        sources[1] += [theirs[b][2], mine[b][2], theirs[b][1], mine[b][1]]
        sources[2] += [mine[b][2], theirs[b][2], mine[b][3], theirs[b][3]]
        sources[3] += [four[b], theirs[b][3], mine[b][3]]
    return merge((0, 1, 2, 3), place, kept, other, children, sum(sources, []), None)


def solution(mesh):
    in_specs = (P("pair", "sib", "tile", None),)
    out_specs = P("pair", ("sib", "tile"), None)
    return jax.shard_map(shards, mesh=mesh, in_specs=in_specs, out_specs=out_specs, check_vma=False)
```

```python
import functools

import jax
import jax.numpy as jnp
from jax import lax
from jax.experimental import pallas as pl
from jax.experimental.pallas import tpu as pltpu
from jax.sharding import PartitionSpec as P

EDGE = 512
OUT_BLK = 192
EDGE_BLK = 64
N_TILE = 8
LANES = 128
F32 = jnp.float32
HIGHEST = lax.Precision.HIGHEST
PARAMS = pltpu.CompilerParams(vmem_limit_bytes=60 * 1024 * 1024)
SMEM = pl.BlockSpec(memory_space=pltpu.SMEM)
VMEM = pl.BlockSpec(memory_space=pltpu.VMEM)
HBM = pl.BlockSpec(memory_space=pl.ANY)


def dot_full(a, b):
    return jnp.dot(a, b, precision=HIGHEST, preferred_element_type=F32)


def split(x):
    high = x.astype(jnp.bfloat16)
    return high, (x - high.astype(F32)).astype(jnp.bfloat16)


def dot_split(a, b):
    a_high, a_low = split(a)
    b_high, b_low = split(b)
    low = jnp.dot(a_low, b_high, preferred_element_type=F32) + jnp.dot(a_high, b_low, preferred_element_type=F32)
    return low + jnp.dot(a_high, b_high, preferred_element_type=F32)


def extract_kernel(place_ref, children_ref, coupling_ref, edge_ref, tiles, sems):
    sib = place_ref[0]
    copies = []
    for pair in range(2):
        for block in range(N_TILE):
            copies.append(
                pltpu.make_async_copy(
                    children_ref.at[pair, :, pl.ds(256 * block + LANES, LANES)],
                    tiles.at[pair, block],
                    sems.at[pair, block],
                )
            )
    for copy in copies:
        copy.start()
    lane = lax.broadcasted_iota(jnp.int32, (256, LANES), 1)
    for pair in range(2):
        position = sib if pair == 0 else 1 - sib
        for half in range(N_TILE // 2):
            copies[pair * N_TILE + 2 * half].wait()
            copies[pair * N_TILE + 2 * half + 1].wait()
            first = pltpu.roll(tiles[pair, 2 * half], 64, 1)
            both = jnp.where(lane < 64, first, tiles[pair, 2 * half + 1])
            columns = pl.ds(LANES * half, LANES)
            coupling_ref[pair, :, columns] = both[:OUT_BLK]
            edge_ref[position, :, columns] = both[OUT_BLK:]


def extract(place, children):
    return pl.pallas_call(
        extract_kernel,
        out_shape=[
            jax.ShapeDtypeStruct((2, OUT_BLK, EDGE), F32),
            jax.ShapeDtypeStruct((2, EDGE_BLK, EDGE), F32),
        ],
        in_specs=[SMEM, HBM],
        out_specs=[VMEM, VMEM],
        scratch_shapes=[
            pltpu.VMEM((2, N_TILE, 256, LANES), F32),
            pltpu.SemaphoreType.DMA((2, N_TILE)),
        ],
        compiler_params=PARAMS,
        cost_estimate=pl.CostEstimate(flops=1000, bytes_accessed=1000, transcendentals=0),
        name="extract",
    )(place, children)


def along(x, k):
    return jnp.broadcast_to(x[:, k : k + 1], x.shape)


def down(x, a):
    return jnp.broadcast_to(x[a : a + 1, :], x.shape)


def inverse_128(rows):
    rows = list(rows)
    lane = lax.broadcasted_iota(jnp.int32, (8, LANES), 1)
    sublane = lax.broadcasted_iota(jnp.int32, (8, LANES), 0)
    for g in range(16):
        k = 8 * g
        pivot_rows = rows[g]
        spread = [along(pivot_rows, k + b) for b in range(8)]
        m = [[down(spread[b], a) for b in range(a + 1)] for a in range(8)]
        in_pivot = (lane >= k) & (lane < k + 8)
        r = [
            jnp.where(lane == k + a, -1.0, jnp.where(in_pivot, 0.0, down(pivot_rows, a)))
            for a in range(8)
        ]
        scale = [None] * 8
        low = [[None] * 8 for _ in range(8)]
        for c in range(8):
            scale[c] = 1.0 / m[c][c]
            for a in range(c + 1, 8):
                low[a][c] = m[a][c] * scale[c]
            for a in range(c + 1, 8):
                for b in range(c + 1, a + 1):
                    m[a][b] = m[a][b] - low[a][c] * m[b][c]
            for a in range(c + 1, 8):
                r[a] = r[a] - low[a][c] * r[c]
        q = [r[a] * scale[a] for a in range(8)]
        for c in range(7, -1, -1):
            for a in range(c):
                q[a] = q[a] - low[c][a] * q[c]
        for i in range(16):
            if i == g:
                continue
            old = rows[i]
            new = jnp.where(in_pivot, 0.0, old)
            for b in range(8):
                new = new - along(old, k + b) * q[b]
            rows[i] = new
        solved = q[0]
        for a in range(1, 8):
            solved = jnp.where(sublane == a, q[a], solved)
        rows[g] = solved
    return [-x for x in rows]


def block_of(tile, k):
    odd = lax.rem(tile, 2)
    toward = 1 - 2 * odd
    shift = [0, -toward, toward, 2][k]
    return lax.rem(lax.div(tile, 2) + shift + 4, 4)


def eliminate_kernel(k, place_ref, *refs):
    rows, panel = refs[-2:]
    sib, tile = place_ref[0], place_ref[1]
    odd = lax.rem(tile, 2)
    match = (sib + odd) != 1
    clash = (sib + odd) == 1

    def put(slot, value):
        rows[pl.ds(pl.multiple_of(slot * EDGE_BLK, EDGE_BLK), EDGE_BLK), :] = value

    def pick(ring, cross, own_way):
        return jnp.where(own_way, ring[0], cross[...])

    if k == 0:
        edges, ring1, cross1, state_out = refs[:-2]
        put(odd, edges[0])
        put(1 - odd, pick(ring1, cross1, match))
    elif k == 1:
        ring1, cross1, ring2, cross2, state_in, state_out = refs[:-2]
        put(odd, pick(ring2, cross2, clash))
        put(1 - odd, pick(ring1, cross1, clash))
    elif k == 2:
        ring2, cross2, ring3, cross3, state_in, state_out = refs[:-2]
        put(odd, pick(ring2, cross2, match))
        put(1 - odd, pick(ring3, cross3, match))
    else:
        ring3, cross3, last, state_in, part_ref, factor_ref, kept_ref, sent_ref = refs[:-2]
        put(odd, last[...])
        put(1 - odd, pick(ring3, cross3, clash))

    block = lax.broadcasted_iota(jnp.int32, (1, EDGE), 1) // LANES
    here = block_of(tile, k)
    columns = pl.ds(pl.multiple_of(here * LANES, LANES), LANES)
    if k == 0:
        panel[...] = rows[...]
    else:
        seen = block == block_of(tile, 0)
        for j in range(1, k):
            seen = seen | (block == block_of(tile, j))
        panel[...] = jnp.where(seen, 0.0, rows[...]) - dot_full(seen_columns(tile, k, rows), state_in[...])
    pivot = panel[:, columns]
    inverse = jnp.concatenate(inverse_128([pivot[8 * i : 8 * i + 8] for i in range(16)]), axis=0)
    row = lax.broadcasted_iota(jnp.int32, (LANES, LANES), 0)
    col = lax.broadcasted_iota(jnp.int32, (LANES, LANES), 1)
    panel[:, columns] = jnp.where(row == col, 1.0, 0.0)
    if k == 3:
        factor = dot_full(factor_ref[...], inverse)
        weights = part_ref[...] + dot_split(factor, panel[...])
        kept_ref[...] = weights[:OUT_BLK]
        sent_ref[...] = weights[OUT_BLK:]
        return
    scaled = dot_full(inverse, panel[...])
    if k > 0:
        done = k * LANES
        state_out[0:done] = jnp.where(block == here, 0.0, state_in[...]) - dot_full(state_in[:, columns], scaled)
    state_out[k * LANES : (k + 1) * LANES] = scaled


def seen_columns(tile, k, ref):
    parts = [ref[:, pl.ds(pl.multiple_of(block_of(tile, j) * LANES, LANES), LANES)] for j in range(k)]
    return jnp.concatenate(parts, axis=1)


def eliminate(k, place, *operands):
    if k < 3:
        out_shape = [jax.ShapeDtypeStruct(((k + 1) * LANES, EDGE), F32)]
    else:
        out_shape = [jax.ShapeDtypeStruct((OUT_BLK, EDGE), F32)] * 2
    return pl.pallas_call(
        functools.partial(eliminate_kernel, k),
        out_shape=out_shape,
        in_specs=[SMEM] + [VMEM] * len(operands),
        out_specs=[VMEM] * len(out_shape),
        scratch_shapes=[pltpu.VMEM((LANES, EDGE), F32)] * 2,
        compiler_params=PARAMS,
        cost_estimate=pl.CostEstimate(flops=1000, bytes_accessed=1000, transcendentals=0),
        name=f"eliminate{k}",
    )(place, *operands)


def part_kernel(place_ref, state_ref, coupling_ref, other_ref, part_ref, factor_ref):
    sib, tile = place_ref[0], place_ref[1]
    here = block_of(tile, 3)
    block = lax.broadcasted_iota(jnp.int32, (1, EDGE), 1) // LANES
    columns = pl.ds(pl.multiple_of(here * LANES, LANES), LANES)
    for i, ref in enumerate((coupling_ref.at[sib], other_ref.at[sib])):
        rows = pl.ds(i * OUT_BLK, OUT_BLK)
        part_ref[rows] = dot_split(seen_columns(tile, 3, ref), state_ref[...])
        factor_ref[rows] = ref[:, columns] - part_ref[rows, columns]
    part_ref[...] = jnp.where(block == here, 0.0, part_ref[...])


def part_weights(place, *operands):
    return pl.pallas_call(
        part_kernel,
        out_shape=[
            jax.ShapeDtypeStruct((2 * OUT_BLK, EDGE), F32),
            jax.ShapeDtypeStruct((2 * OUT_BLK, LANES), F32),
        ],
        in_specs=[SMEM] + [VMEM] * 3,
        out_specs=[VMEM] * 2,
        compiler_params=PARAMS,
        cost_estimate=pl.CostEstimate(flops=1000, bytes_accessed=1000, transcendentals=0),
        name="part_weights",
    )(place, *operands)


def dot_rows(a, b):
    return lax.dot_general(a, b, (((1,), (1,)), ((), ())), preferred_element_type=F32)


def merge_kernel(blocks, place_ref, kept_ref, other_ref, children_ref, *refs):
    out_ref, points, own, result, point_sems, own_sems, out_sems = refs[-7:]
    sources = list(refs[:-7])
    sib, tile = place_ref[0], place_ref[1]
    odd = lax.rem(tile, 2)
    match = (sib + odd) == 1

    def fetch(at, box, slot, pair, source):
        return pltpu.make_async_copy(
            source.at[pair],
            points.at[at, box, pair, pl.ds(pl.multiple_of(slot * OUT_BLK, OUT_BLK), OUT_BLK), :],
            point_sems.at[at, box, pair, slot],
        )

    def own_copy(at, pair):
        first = pl.multiple_of(512 * block_of(tile, blocks[at]), 512)
        return pltpu.make_async_copy(
            children_ref.at[pair, pl.ds(0, OUT_BLK), pl.ds(first, 512)], own.at[at, pair], own_sems.at[at, pair]
        )

    for at, k in enumerate(blocks):
        for box in range(2):
            choices = [sources.pop(0) for _ in range(4 if k in (1, 2) else 3)]
            choices = [choices[:-2], choices[-2:]]
            for pair in range(2):
                for slot, candidates in ((odd, choices[0]), (1 - odd, choices[1])):
                    if len(candidates) == 1:
                        fetch(at, box, slot, pair, candidates[0]).start()
                    else:

                        @pl.when(match)
                        def _():
                            fetch(at, box, slot, pair, candidates[0]).start()

                        @pl.when(jnp.logical_not(match))
                        def _():
                            fetch(at, box, slot, pair, candidates[1]).start()

                if box == 0:
                    own_copy(at, pair).start()

    weights = [split(jnp.where(sib == pair, kept_ref[...], other_ref[...])) for pair in range(2)]
    writes = []
    for at, k in enumerate(blocks):
        for box in range(2):
            for pair in range(2):
                weight_high, weight_low = weights[pair]
                for slot in range(2):
                    fetch(at, box, slot, pair, refs[0]).wait()
                points_high, points_low = split(points[at, box, pair])
                both = dot_rows(jnp.concatenate([weight_high, weight_low], axis=0), points_high)
                term = (both[OUT_BLK:] + dot_rows(weight_high, points_low)) + both[:OUT_BLK]
                if box == 0:
                    own_copy(at, pair).wait()
                    diagonal = own[at, pair]
                    term = term - jnp.concatenate([diagonal[:, :OUT_BLK], diagonal[:, 256 : 256 + OUT_BLK]], axis=1)
                result[at, box, pair] = -term
                which = sib if box == 0 else 1 - sib
                columns = pl.multiple_of((4 * which + block_of(tile, k)) * 2 * OUT_BLK, 2 * OUT_BLK)
                write = pltpu.make_async_copy(
                    result.at[at, box, pair],
                    out_ref.at[pair, :, pl.ds(columns, 2 * OUT_BLK)],
                    out_sems.at[at, box, pair],
                )
                write.start()
                writes.append(write)
    for write in writes:
        write.wait()


def merge(blocks, place, kept, other, children, sources, out):
    operands = [place, kept, other, children, *sources]
    specs = [SMEM, VMEM, VMEM] + [HBM] * (1 + len(sources))
    aliases = {}
    if out is not None:
        aliases = {len(operands): 0}
        operands.append(out)
        specs.append(HBM)
    n = len(blocks)
    return pl.pallas_call(
        functools.partial(merge_kernel, blocks),
        out_shape=jax.ShapeDtypeStruct((2, OUT_BLK, 2 * N_TILE * OUT_BLK), F32),
        in_specs=specs,
        out_specs=HBM,
        scratch_shapes=[
            pltpu.VMEM((n, 2, 2, 2 * OUT_BLK, EDGE), F32),
            pltpu.VMEM((n, 2, OUT_BLK, 512), F32),
            pltpu.VMEM((n, 2, 2, OUT_BLK, 2 * OUT_BLK), F32),
            pltpu.SemaphoreType.DMA((n, 2, 2, 2)),
            pltpu.SemaphoreType.DMA((n, 2)),
            pltpu.SemaphoreType.DMA((n, 2, 2)),
        ],
        input_output_aliases=aliases,
        compiler_params=PARAMS,
        cost_estimate=pl.CostEstimate(flops=1000, bytes_accessed=1000, transcendentals=0),
        name="merge" + "".join(map(str, blocks)),
    )(*operands)


def tie(*arrays):
    return lax.optimization_barrier(arrays)


def shards(children):
    sib, tile = lax.axis_index("sib"), lax.axis_index("tile")
    place = jnp.stack([sib, tile]).astype(jnp.int32)
    children = children[:, 0]
    around = [(t, (t + 1) % N_TILE) for t in range(N_TILE)]
    around += [(N_TILE + t, N_TILE + (t - 1) % N_TILE) for t in range(N_TILE)]
    against = [(to, source) for source, to in around]

    def swap(x):
        return lax.ppermute(x, "sib", [(0, 1), (1, 0)])

    def pass_on(x):
        return lax.ppermute(x, ("sib", "tile"), around)

    def pass_edges(x):
        return lax.ppermute(x, ("sib", "tile"), against)

    coupling, edge = extract(place, children)
    edges = edge + swap(edge)[::-1]
    own_box = [coupling, pass_on(coupling)]
    other_box = [swap(coupling)]
    other_box.append(pass_on(other_box[0]))
    ring, cross = [edges, pass_edges(edges)], [None]
    ring.append(pass_edges(ring[1]))
    cross.append(swap(ring[1][1]))
    cross[1], own_box[1] = tie(cross[1], own_box[1])
    own_box.append(pass_on(own_box[1]))
    state = eliminate(0, place, edges, ring[1], cross[1])[0]
    state, ring[2], other_box[1] = tie(state, ring[2], other_box[1])
    ring.append(pass_edges(ring[2]))
    cross.append(swap(ring[2][1]))
    other_box.append(pass_on(other_box[1]))
    state = eliminate(1, place, ring[1], cross[1], ring[2], cross[2], state)[0]
    state, ring[3], own_box[2] = tie(state, ring[3], own_box[2])
    last = pass_edges(ring[3][0])
    cross.append(swap(ring[3][1]))
    own_box.append(pass_on(own_box[2]))
    state = eliminate(2, place, ring[2], cross[2], ring[3], cross[3], state)[0]
    state, last, other_box[2] = tie(state, last, other_box[2])
    other_box.append(pass_on(other_box[2]))
    part, factor = part_weights(place, state, coupling, other_box[0])
    part, own_box[3] = tie(part, own_box[3])
    own_box.append(pass_on(own_box[3]))
    kept, sent = eliminate(3, place, ring[3], cross[3], last, state, part, factor)
    kept, sent, own_box[4] = tie(kept, sent, own_box[4])
    other = swap(sent)
    own_cross = [None] + [swap(own_box[d]) for d in range(1, 5)]
    other_cross = [None] + [swap(other_box[d]) for d in range(1, 4)]

    mine = [own_box, other_box]
    theirs = [other_cross, own_cross]
    zero = [coupling, other_box[0]]
    four = [own_box[4], own_cross[4]]
    sources = [[], [], [], []]
    for b in range(2):
        sources[0] += [zero[b], mine[b][1], theirs[b][1]]
        sources[1] += [theirs[b][2], mine[b][2], theirs[b][1], mine[b][1]]
        sources[2] += [mine[b][2], theirs[b][2], mine[b][3], theirs[b][3]]
        sources[3] += [four[b], theirs[b][3], mine[b][3]]
    return merge((0, 1, 2, 3), place, kept, other, children, sum(sources, []), None)


def solution(mesh):
    in_specs = (P("pair", "sib", "tile", None),)
    out_specs = P("pair", ("sib", "tile"), None)
    return jax.shard_map(shards, mesh=mesh, in_specs=in_specs, out_specs=out_specs, check_vma=False)
```

```python
import functools

import jax
import jax.numpy as jnp
from jax import lax
from jax.experimental import pallas as pl
from jax.experimental.pallas import tpu as pltpu
from jax.sharding import PartitionSpec as P

EDGE = 512
OUT_BLK = 192
EDGE_BLK = 64
N_TILE = 8
LANES = 128
F32 = jnp.float32
HIGHEST = lax.Precision.HIGHEST
PARAMS = pltpu.CompilerParams(vmem_limit_bytes=60 * 1024 * 1024)
SMEM = pl.BlockSpec(memory_space=pltpu.SMEM)
VMEM = pl.BlockSpec(memory_space=pltpu.VMEM)
HBM = pl.BlockSpec(memory_space=pl.ANY)


def dot_full(a, b):
    return jnp.dot(a, b, precision=HIGHEST, preferred_element_type=F32)


def split(x):
    high = x.astype(jnp.bfloat16)
    return high, (x - high.astype(F32)).astype(jnp.bfloat16)


def dot_split(a, b):
    a_high, a_low = split(a)
    b_high, b_low = split(b)
    low = jnp.dot(a_low, b_high, preferred_element_type=F32) + jnp.dot(a_high, b_low, preferred_element_type=F32)
    return low + jnp.dot(a_high, b_high, preferred_element_type=F32)


def extract_kernel(place_ref, children_ref, coupling_ref, edge_ref, tiles, sems):
    sib = place_ref[0]
    copies = []
    for pair in range(2):
        for block in range(N_TILE):
            copies.append(
                pltpu.make_async_copy(
                    children_ref.at[pair, :, pl.ds(256 * block + LANES, LANES)],
                    tiles.at[pair, block],
                    sems.at[pair, block],
                )
            )
    for copy in copies:
        copy.start()
    lane = lax.broadcasted_iota(jnp.int32, (256, LANES), 1)
    for pair in range(2):
        position = sib if pair == 0 else 1 - sib
        for half in range(N_TILE // 2):
            copies[pair * N_TILE + 2 * half].wait()
            copies[pair * N_TILE + 2 * half + 1].wait()
            first = pltpu.roll(tiles[pair, 2 * half], 64, 1)
            both = jnp.where(lane < 64, first, tiles[pair, 2 * half + 1])
            columns = pl.ds(LANES * half, LANES)
            coupling_ref[pair, :, columns] = both[:OUT_BLK]
            edge_ref[position, :, columns] = both[OUT_BLK:]


def extract(place, children):
    return pl.pallas_call(
        extract_kernel,
        out_shape=[
            jax.ShapeDtypeStruct((2, OUT_BLK, EDGE), F32),
            jax.ShapeDtypeStruct((2, EDGE_BLK, EDGE), F32),
        ],
        in_specs=[SMEM, HBM],
        out_specs=[VMEM, VMEM],
        scratch_shapes=[
            pltpu.VMEM((2, N_TILE, 256, LANES), F32),
            pltpu.SemaphoreType.DMA((2, N_TILE)),
        ],
        compiler_params=PARAMS,
        cost_estimate=pl.CostEstimate(flops=1000, bytes_accessed=1000, transcendentals=0),
        name="extract",
    )(place, children)


def along(x, k):
    return jnp.broadcast_to(x[:, k : k + 1], x.shape)


def down(x, a):
    return jnp.broadcast_to(x[a : a + 1, :], x.shape)


def inverse_128(rows):
    rows = list(rows)
    lane = lax.broadcasted_iota(jnp.int32, (8, LANES), 1)
    sublane = lax.broadcasted_iota(jnp.int32, (8, LANES), 0)
    for g in range(16):
        k = 8 * g
        pivot_rows = rows[g]
        spread = [along(pivot_rows, k + b) for b in range(8)]
        m = [[down(spread[b], a) for b in range(a + 1)] for a in range(8)]
        in_pivot = (lane >= k) & (lane < k + 8)
        r = [
            jnp.where(lane == k + a, -1.0, jnp.where(in_pivot, 0.0, down(pivot_rows, a)))
            for a in range(8)
        ]
        scale = [None] * 8
        low = [[None] * 8 for _ in range(8)]
        for c in range(8):
            scale[c] = 1.0 / m[c][c]
            for a in range(c + 1, 8):
                low[a][c] = m[a][c] * scale[c]
            for a in range(c + 1, 8):
                for b in range(c + 1, a + 1):
                    m[a][b] = m[a][b] - low[a][c] * m[b][c]
            for a in range(c + 1, 8):
                r[a] = r[a] - low[a][c] * r[c]
        q = [r[a] * scale[a] for a in range(8)]
        for c in range(7, -1, -1):
            for a in range(c):
                q[a] = q[a] - low[c][a] * q[c]
        for i in range(16):
            if i == g:
                continue
            old = rows[i]
            new = jnp.where(in_pivot, 0.0, old)
            for b in range(8):
                new = new - along(old, k + b) * q[b]
            rows[i] = new
        solved = q[0]
        for a in range(1, 8):
            solved = jnp.where(sublane == a, q[a], solved)
        rows[g] = solved
    return [-x for x in rows]


def block_of(tile, k):
    odd = lax.rem(tile, 2)
    toward = 1 - 2 * odd
    shift = [0, -toward, toward, 2][k]
    return lax.rem(lax.div(tile, 2) + shift + 4, 4)


def eliminate_kernel(k, place_ref, *refs):
    rows, panel = refs[-2:]
    sib, tile = place_ref[0], place_ref[1]
    odd = lax.rem(tile, 2)
    match = (sib + odd) != 1
    clash = (sib + odd) == 1

    def put(slot, value):
        rows[pl.ds(pl.multiple_of(slot * EDGE_BLK, EDGE_BLK), EDGE_BLK), :] = value

    def pick(ring, cross, own_way):
        return jnp.where(own_way, ring[0], cross[...])

    if k == 0:
        edges, ring1, cross1, state_out = refs[:-2]
        put(odd, edges[0])
        put(1 - odd, pick(ring1, cross1, match))
    elif k == 1:
        ring1, cross1, ring2, cross2, state_in, state_out = refs[:-2]
        put(odd, pick(ring2, cross2, clash))
        put(1 - odd, pick(ring1, cross1, clash))
    elif k == 2:
        ring2, cross2, ring3, cross3, state_in, state_out = refs[:-2]
        put(odd, pick(ring2, cross2, match))
        put(1 - odd, pick(ring3, cross3, match))
    else:
        ring3, cross3, last, state_in, part_ref, factor_ref, kept_ref, sent_ref = refs[:-2]
        put(odd, last[...])
        put(1 - odd, pick(ring3, cross3, clash))

    block = lax.broadcasted_iota(jnp.int32, (1, EDGE), 1) // LANES
    here = block_of(tile, k)
    columns = pl.ds(pl.multiple_of(here * LANES, LANES), LANES)
    if k == 0:
        panel[...] = rows[...]
    else:
        seen = block == block_of(tile, 0)
        for j in range(1, k):
            seen = seen | (block == block_of(tile, j))
        panel[...] = jnp.where(seen, 0.0, rows[...]) - dot_full(seen_columns(tile, k, rows), state_in[...])
    pivot = panel[:, columns]
    inverse = jnp.concatenate(inverse_128([pivot[8 * i : 8 * i + 8] for i in range(16)]), axis=0)
    row = lax.broadcasted_iota(jnp.int32, (LANES, LANES), 0)
    col = lax.broadcasted_iota(jnp.int32, (LANES, LANES), 1)
    panel[:, columns] = jnp.where(row == col, 1.0, 0.0)
    if k == 3:
        factor = dot_full(factor_ref[...], inverse)
        weights = part_ref[...] + dot_split(factor, panel[...])
        kept_ref[...] = weights[:OUT_BLK]
        sent_ref[...] = weights[OUT_BLK:]
        return
    scaled = dot_full(inverse, panel[...])
    if k > 0:
        done = k * LANES
        state_out[0:done] = jnp.where(block == here, 0.0, state_in[...]) - dot_full(state_in[:, columns], scaled)
    state_out[k * LANES : (k + 1) * LANES] = scaled


def seen_columns(tile, k, ref):
    parts = [ref[:, pl.ds(pl.multiple_of(block_of(tile, j) * LANES, LANES), LANES)] for j in range(k)]
    return jnp.concatenate(parts, axis=1)


def eliminate(k, place, *operands):
    if k < 3:
        out_shape = [jax.ShapeDtypeStruct(((k + 1) * LANES, EDGE), F32)]
    else:
        out_shape = [jax.ShapeDtypeStruct((OUT_BLK, EDGE), F32)] * 2
    return pl.pallas_call(
        functools.partial(eliminate_kernel, k),
        out_shape=out_shape,
        in_specs=[SMEM] + [VMEM] * len(operands),
        out_specs=[VMEM] * len(out_shape),
        scratch_shapes=[pltpu.VMEM((LANES, EDGE), F32)] * 2,
        compiler_params=PARAMS,
        cost_estimate=pl.CostEstimate(flops=1000, bytes_accessed=1000, transcendentals=0),
        name=f"eliminate{k}",
    )(place, *operands)


def part_kernel(place_ref, state_ref, coupling_ref, other_ref, part_ref, factor_ref):
    sib, tile = place_ref[0], place_ref[1]
    here = block_of(tile, 3)
    block = lax.broadcasted_iota(jnp.int32, (1, EDGE), 1) // LANES
    columns = pl.ds(pl.multiple_of(here * LANES, LANES), LANES)
    for i, ref in enumerate((coupling_ref.at[sib], other_ref.at[sib])):
        rows = pl.ds(i * OUT_BLK, OUT_BLK)
        part_ref[rows] = dot_split(seen_columns(tile, 3, ref), state_ref[...])
        factor_ref[rows] = ref[:, columns] - part_ref[rows, columns]
    part_ref[...] = jnp.where(block == here, 0.0, part_ref[...])


def part_weights(place, *operands):
    return pl.pallas_call(
        part_kernel,
        out_shape=[
            jax.ShapeDtypeStruct((2 * OUT_BLK, EDGE), F32),
            jax.ShapeDtypeStruct((2 * OUT_BLK, LANES), F32),
        ],
        in_specs=[SMEM] + [VMEM] * 3,
        out_specs=[VMEM] * 2,
        compiler_params=PARAMS,
        cost_estimate=pl.CostEstimate(flops=1000, bytes_accessed=1000, transcendentals=0),
        name="part_weights",
    )(place, *operands)


def dot_rows(a, b):
    return lax.dot_general(a, b, (((1,), (1,)), ((), ())), preferred_element_type=F32)


def merge_kernel(blocks, place_ref, kept_ref, other_ref, children_ref, *refs):
    out_ref, points, own, result, point_sems, own_sems, out_sems = refs[-7:]
    sources = list(refs[:-7])
    sib, tile = place_ref[0], place_ref[1]
    odd = lax.rem(tile, 2)
    match = (sib + odd) == 1

    def fetch(at, box, slot, pair, source):
        return pltpu.make_async_copy(
            source.at[pair],
            points.at[at, box, pair, pl.ds(pl.multiple_of(slot * OUT_BLK, OUT_BLK), OUT_BLK), :],
            point_sems.at[at, box, pair, slot],
        )

    def own_copy(at, pair):
        first = pl.multiple_of(512 * block_of(tile, blocks[at]), 512)
        return pltpu.make_async_copy(
            children_ref.at[pair, pl.ds(0, OUT_BLK), pl.ds(first, 512)], own.at[at, pair], own_sems.at[at, pair]
        )

    for at, k in enumerate(blocks):
        for box in range(2):
            choices = [sources.pop(0) for _ in range(4 if k in (1, 2) else 3)]
            choices = [choices[:-2], choices[-2:]]
            for pair in range(2):
                for slot, candidates in ((odd, choices[0]), (1 - odd, choices[1])):
                    if len(candidates) == 1:
                        fetch(at, box, slot, pair, candidates[0]).start()
                    else:

                        @pl.when(match)
                        def _():
                            fetch(at, box, slot, pair, candidates[0]).start()

                        @pl.when(jnp.logical_not(match))
                        def _():
                            fetch(at, box, slot, pair, candidates[1]).start()

                if box == 0:
                    own_copy(at, pair).start()

    weights = [split(jnp.where(sib == pair, kept_ref[...], other_ref[...])) for pair in range(2)]
    writes = []
    for at, k in enumerate(blocks):
        for box in range(2):
            for pair in range(2):
                weight_high, weight_low = weights[pair]
                for slot in range(2):
                    fetch(at, box, slot, pair, refs[0]).wait()
                points_high, points_low = split(points[at, box, pair])
                both = dot_rows(jnp.concatenate([weight_high, weight_low], axis=0), points_high)
                term = (both[OUT_BLK:] + dot_rows(weight_high, points_low)) + both[:OUT_BLK]
                if box == 0:
                    own_copy(at, pair).wait()
                    diagonal = own[at, pair]
                    term = term - jnp.concatenate([diagonal[:, :OUT_BLK], diagonal[:, 256 : 256 + OUT_BLK]], axis=1)
                result[at, box, pair] = -term
                which = sib if box == 0 else 1 - sib
                columns = pl.multiple_of((4 * which + block_of(tile, k)) * 2 * OUT_BLK, 2 * OUT_BLK)
                write = pltpu.make_async_copy(
                    result.at[at, box, pair],
                    out_ref.at[pair, :, pl.ds(columns, 2 * OUT_BLK)],
                    out_sems.at[at, box, pair],
                )
                write.start()
                writes.append(write)
    for write in writes:
        write.wait()


def merge(blocks, place, kept, other, children, sources, out):
    operands = [place, kept, other, children, *sources]
    specs = [SMEM, VMEM, VMEM] + [HBM] * (1 + len(sources))
    aliases = {}
    if out is not None:
        aliases = {len(operands): 0}
        operands.append(out)
        specs.append(HBM)
    n = len(blocks)
    return pl.pallas_call(
        functools.partial(merge_kernel, blocks),
        out_shape=jax.ShapeDtypeStruct((2, OUT_BLK, 2 * N_TILE * OUT_BLK), F32),
        in_specs=specs,
        out_specs=HBM,
        scratch_shapes=[
            pltpu.VMEM((n, 2, 2, 2 * OUT_BLK, EDGE), F32),
            pltpu.VMEM((n, 2, OUT_BLK, 512), F32),
            pltpu.VMEM((n, 2, 2, OUT_BLK, 2 * OUT_BLK), F32),
            pltpu.SemaphoreType.DMA((n, 2, 2, 2)),
            pltpu.SemaphoreType.DMA((n, 2)),
            pltpu.SemaphoreType.DMA((n, 2, 2)),
        ],
        input_output_aliases=aliases,
        compiler_params=PARAMS,
        cost_estimate=pl.CostEstimate(flops=1000, bytes_accessed=1000, transcendentals=0),
        name="merge" + "".join(map(str, blocks)),
    )(*operands)


def tie(*arrays):
    return lax.optimization_barrier(arrays)


def shards(children):
    sib, tile = lax.axis_index("sib"), lax.axis_index("tile")
    place = jnp.stack([sib, tile]).astype(jnp.int32)
    children = children[:, 0]
    around = [(t, (t + 1) % N_TILE) for t in range(N_TILE)]
    around += [(N_TILE + t, N_TILE + (t - 1) % N_TILE) for t in range(N_TILE)]
    against = [(to, source) for source, to in around]

    def swap(x):
        return lax.ppermute(x, "sib", [(0, 1), (1, 0)])

    def pass_on(x):
        return lax.ppermute(x, ("sib", "tile"), around)

    def pass_edges(x):
        return lax.ppermute(x, ("sib", "tile"), against)

    coupling, edge = extract(place, children)
    edges = edge + swap(edge)[::-1]
    own_box = [coupling, pass_on(coupling)]
    other_box = [swap(coupling)]
    other_box.append(pass_on(other_box[0]))
    ring, cross = [edges, pass_edges(edges)], [None]
    ring.append(pass_edges(ring[1]))
    cross.append(swap(ring[1][1]))
    cross[1], own_box[1] = tie(cross[1], own_box[1])
    own_box.append(pass_on(own_box[1]))
    state = eliminate(0, place, edges, ring[1], cross[1])[0]
    state, ring[2], other_box[1] = tie(state, ring[2], other_box[1])
    ring.append(pass_edges(ring[2]))
    cross.append(swap(ring[2][1]))
    other_box.append(pass_on(other_box[1]))
    state = eliminate(1, place, ring[1], cross[1], ring[2], cross[2], state)[0]
    state, ring[3], own_box[2] = tie(state, ring[3], own_box[2])
    last = pass_edges(ring[3][0])
    cross.append(swap(ring[3][1]))
    own_box.append(pass_on(own_box[2]))
    state = eliminate(2, place, ring[2], cross[2], ring[3], cross[3], state)[0]
    state, last, other_box[2], own_box[3] = tie(state, last, other_box[2], own_box[3])
    own_box.append(pass_on(own_box[3]))
    other_box.append(pass_on(other_box[2]))
    part, factor = part_weights(place, state, coupling, other_box[0])
    kept, sent = eliminate(3, place, ring[3], cross[3], last, state, part, factor)
    kept, sent, own_box[4] = tie(kept, sent, own_box[4])
    other = swap(sent)
    farthest = swap(own_box[4])
    own_cross = [None] + [swap(own_box[d]) for d in range(1, 4)]
    other_cross = [None] + [swap(other_box[d]) for d in range(1, 4)]

    mine = [own_box, other_box]
    theirs = [other_cross, own_cross]
    zero = [coupling, other_box[0]]
    sources = [[], [], [], []]
    for b in range(2):
        sources[0] += [zero[b], mine[b][1], theirs[b][1]]
        sources[1] += [theirs[b][2], mine[b][2], theirs[b][1], mine[b][1]]
    out = merge((0, 1), place, kept, other, children, sources[0] + sources[1], None)
    four = [own_box[4], farthest]
    for b in range(2):
        sources[2] += [mine[b][2], theirs[b][2], mine[b][3], theirs[b][3]]
        sources[3] += [four[b], theirs[b][3], mine[b][3]]
    return merge((2, 3), place, kept, other, children, sources[2] + sources[3], out)


def solution(mesh):
    in_specs = (P("pair", "sib", "tile", None),)
    out_specs = P("pair", ("sib", "tile"), None)
    return jax.shard_map(shards, mesh=mesh, in_specs=in_specs, out_specs=out_specs, check_vma=False)
```
